32 devices in a mesh: section: 8 (over z, x), dp: 4 (over y, core).
Axes of the slice: x: 2, y: 2, z: 4, core: 2. Of those that a mesh axis runs over, the one named last changes fastest.
Arguments:
- states: bfloat16 [4, 8, 32, 4096], P('dp', 'section'), may hold values from -8 to 8
- memory: bfloat16 [4, 8, 2, 128, 4096], P('dp', 'section'), may hold values from -12 to 12
- memory_len: int32 [4, 8], P('dp', 'section'), may hold values from 2 to 128
- decode_len: int32 [4, 8], P('dp', 'section'), may hold values from 1 to 32
- owner_map: int32 [8], replicated, may hold values from 0 to 7, as said below
- section_gain: bfloat16 [8, 4096], P('section'), may hold values from 0.5 to 2
- cotangent: bfloat16 [4, 3, 8, 32, 4096], P('dp', None, 'section'), may hold values from -18 to 18
Outputs:
- final_states: bfloat16 [4, 8, 32, 4096], P('dp', 'section')
- gain_grad: float32 [8, 4096], P('section')
The draws below stay inside these ranges and needn't reach their ends.
Inputs may be any that keep to these rules, and one draw needn't show every extreme that they name: owner_map[m] = (m + c) mod 8 for one offset c from 3 to 7, the same for all m.
All inputs are finite; a program needn't handle non-finite values.
Results may differ from the reference program's by a relative error of at most 0.0085.
Values may be sent and summed in bfloat16 or wider, within the bound.
A program may use at most 64 MiB of HBM per device.

```python
import jax
import jax.numpy as jnp
from jax import lax

HEADS = 16
HD = 256
D = 4096
DEC = 32
ENC = 128
STEPS = 3
REPLICAS = 4
SECTIONS = 8


def draw_owner_map(key, part):
    offset = jax.random.randint(jax.random.fold_in(key, 51), (), STEPS, SECTIONS)
    return ((jnp.arange(SECTIONS) + offset) % SECTIONS).astype(jnp.int32)


def draw_states(key, part):
    shape_all = (REPLICAS, SECTIONS, DEC, HEADS * HD)
    own = jax.random.fold_in(key, 21)
    values = jnp.clip(jax.random.normal(own, shape_all, jnp.float32), -6.0, 6.0)
    return values.astype(jnp.bfloat16)


def draw_memory(key, part):
    shape_half = (REPLICAS, SECTIONS, ENC, HEADS * HD)
    key_seed = jax.random.fold_in(key, 31)
    value_seed = jax.random.fold_in(key, 32)
    keys = jnp.clip(2.0 * jax.random.normal(key_seed, shape_half, jnp.float32), -12.0, 12.0).astype(jnp.bfloat16)
    values = jnp.clip(2.0 * jax.random.normal(value_seed, shape_half, jnp.float32), -12.0, 12.0).astype(jnp.bfloat16)
    return jnp.stack([keys, values], axis=2)


def draw_cotangent(key, part):
    shape_all = (REPLICAS, STEPS, SECTIONS, DEC, HEADS * HD)
    own = jax.random.fold_in(key, 41)
    rising = 3.0 ** (jnp.arange(REPLICAS, dtype=jnp.float32) / max(REPLICAS - 1, 1))
    rising = rising.reshape(REPLICAS, 1, 1, 1, 1)
    values = jnp.clip(jax.random.normal(own, shape_all, jnp.float32), -6.0, 6.0)
    return (values * rising).astype(jnp.bfloat16)


def touch_ends(array, stream_key, low, high):
    index_at = [jax.random.randint(jax.random.fold_in(stream_key, axis), (), 0, length) for axis, length in enumerate(array.shape)]
    longest = array.shape.index(max(array.shape))
    next_to = index_at[:longest] + [(index_at[longest] + 1) % array.shape[longest]] + index_at[longest + 1:]
    return array.at[tuple(index_at)].set(low).at[tuple(next_to)].set(high)


def level_of(rng, extent, shards, least, largest):
    loudness, own = 1.0, jax.random.fold_in(rng, 6)
    for axis_at, parts in shards:
        steps = jnp.exp(jax.random.uniform(jax.random.fold_in(own, axis_at), (parts,), jnp.float32, least / len(shards), largest / len(shards)))
        loudness = loudness * jnp.repeat(steps, extent[axis_at] // parts).reshape([-1 if axis == axis_at else 1 for axis in range(len(extent))])
    return loudness


def setup_inputs(seed: int = 0) -> dict:
    key_of = jax.random.split(jax.random.key(seed), 8)
    states = draw_states(jax.random.fold_in(key_of[7], 71), 0)
    memory = draw_memory(jax.random.fold_in(key_of[7], 71), 0)
    memory_len = touch_ends(jax.random.randint(key_of[2], (REPLICAS, SECTIONS), 2, ENC + 1), jax.random.fold_in(key_of[2], 1), 2, ENC).astype(jnp.int32)
    decode_len = touch_ends(jax.random.randint(key_of[3], (REPLICAS, SECTIONS), 1, DEC + 1), jax.random.fold_in(key_of[3], 1), 1, DEC).astype(jnp.int32)
    owner_map = draw_owner_map(jax.random.fold_in(key_of[7], 71), 0)
    section_gain = jnp.clip(0.5 + 1.5 * jax.random.uniform(key_of[5], (SECTIONS, D), jnp.float32) ** level_of(key_of[5], (SECTIONS, D), ((0, 8),), -0.2, 0.2), 0.5, 2.0).astype(jnp.bfloat16)
    cotangent = draw_cotangent(jax.random.fold_in(key_of[7], 71), 0)
    return dict(states=states, memory=memory, memory_len=memory_len, decode_len=decode_len, owner_map=owner_map, section_gain=section_gain, cotangent=cotangent)


def attend(queries, key_rows, value_rows, memory_length):
    sections_here = queries.shape[0]
    query_heads = queries.astype(jnp.float32).reshape(sections_here, DEC, HEADS, HD)
    key_heads = key_rows.astype(jnp.float32).reshape(sections_here, ENC, HEADS, HD)
    value_heads = value_rows.astype(jnp.float32).reshape(sections_here, ENC, HEADS, HD)
    scores = jnp.einsum('sqhd,skhd->shqk', query_heads, key_heads) * HD ** (-0.5)
    key_live = jnp.arange(ENC)[None, :] < memory_length[:, None]
    scores = jnp.where(key_live[:, None, None, :], scores, jnp.float32(-1e+30))
    top = lax.optimization_barrier(jnp.max(scores, axis=-1, keepdims=True))
    expo = jnp.exp(scores - top)
    probs = (expo / lax.optimization_barrier(jnp.sum(expo, axis=-1, keepdims=True))).astype(jnp.bfloat16)
    mixed = jnp.einsum('shqk,skhd->sqhd', probs.astype(jnp.float32), value_heads)
    return mixed.reshape(sections_here, DEC, HEADS * HD).astype(jnp.bfloat16)

def reference(states, memory, memory_len, decode_len, owner_map, section_gain, cotangent):

    def one_replica(pieces):
        current, memory_rep, memory_rep_len, decode_rep_len, cotangent_rep = pieces
        held = memory_rep[owner_map]
        held_len = memory_rep_len[owner_map]
        gain_total = jnp.zeros((SECTIONS, HEADS * HD), jnp.float32)
        live_rows = jnp.arange(DEC)[None, :, None] < decode_rep_len[:, None, None]
        for window_step in range(STEPS):
            state_wide = current.astype(jnp.float32)
            queries = (state_wide * lax.rsqrt(lax.optimization_barrier(jnp.mean(state_wide * state_wide, axis=-1, keepdims=True)) + 1e-06)).astype(jnp.bfloat16)
            attended = attend(queries, held[:, 0], held[:, 1], held_len).astype(jnp.float32)
            gains_now = jnp.roll(section_gain, -window_step, 0).astype(jnp.float32)[:, None, :]
            cot_now = jnp.roll(cotangent_rep[window_step], -window_step, 0).astype(jnp.float32)
            by_batch = lax.optimization_barrier(jnp.sum(jnp.where(live_rows, cot_now * attended, jnp.float32(0.0)), axis=1))
            gain_total = gain_total + jnp.roll(by_batch, window_step, 0)
            current = jnp.where(live_rows, state_wide + gains_now * attended, state_wide).astype(jnp.bfloat16)
        return (jnp.roll(current, STEPS - 1, 0), gain_total)
    finals, totals = lax.map(one_replica, (states, memory, memory_len, decode_len, cotangent))
    return (finals, lax.optimization_barrier(jnp.sum(totals, axis=0)))
```

```python
import functools

import jax
import jax.numpy as jnp
from jax import lax
from jax.experimental import pallas as pl
from jax.experimental.pallas import tpu as pltpu
from jax.sharding import PartitionSpec as P

HD = 256
STEPS = 3
MESH = pl.DeviceIdType.MESH


def window_kernel(
    offset, sections, replicas,
    states, memory, memory_len, decode_len, gain, cotangent,
    final, grad,
    kv, held, cots, mixed, note, notes, rows_f32, part, parts, slots,
    kv_sem, x_send, x_recv, cot_send, cot_recv, note_send, note_recv,
    part_send, part_recv, final_send, final_recv, slot_send, slot_recv,
):
    me = lax.axis_index("section")
    rep = lax.axis_index("dp")
    heads = held.shape[1] // HD
    dec = held.shape[0]
    enc = kv.shape[1]

    def section_at(shift):
        return {"section": lax.rem(me + shift % sections, sections)}

    barrier = pltpu.get_barrier_semaphore()
    shifts = sorted({s % sections for t in range(STEPS) for s in (offset - t, t - offset)})
    for shift in shifts:
        pl.semaphore_signal(barrier, inc=1, device_id=section_at(shift), device_id_type=MESH)

    def greet(j, carry):
        pl.semaphore_signal(
            barrier, inc=1, device_id={"dp": lax.rem(rep + j, replicas)}, device_id_type=MESH
        )
        return carry

    lax.fori_loop(1, replicas, greet, 0)

    kv_copy = pltpu.make_async_copy(memory.at[0, 0], kv, kv_sem)
    kv_copy.start()

    for h in range(heads):
        rows_f32[h : h + 1, :] = gain[:, h * HD : (h + 1) * HD].astype(jnp.float32)
    rows_f32[heads:, :] = jnp.full((heads, HD), decode_len[0, 0], jnp.int32).astype(jnp.float32)
    note[...] = rows_f32[...].astype(jnp.bfloat16)

    pl.semaphore_wait(barrier, len(shifts) + replicas - 1)

    x_copy = pltpu.make_async_remote_copy(
        src_ref=states.at[0, 0], dst_ref=held, send_sem=x_send, recv_sem=x_recv,
        device_id=section_at(offset), device_id_type=MESH,
    )
    x_copy.start()
    note_copies = [
        pltpu.make_async_remote_copy(
            src_ref=note, dst_ref=notes.at[t], send_sem=note_send.at[t],
            recv_sem=note_recv.at[t], device_id=section_at(offset - t), device_id_type=MESH,
        )
        for t in range(STEPS)
    ]
    for copy in note_copies:
        copy.start()
    cot_copies = [
        pltpu.make_async_remote_copy(
            src_ref=cotangent.at[0, t, 0], dst_ref=cots.at[t], send_sem=cot_send.at[t],
            recv_sem=cot_recv.at[t], device_id=section_at(offset - t), device_id_type=MESH,
        )
        for t in range(STEPS)
    ]
    cot_copies[0].start()

    kv_copy.wait()
    x_copy.wait_recv()
    for copy in cot_copies[1:]:
        copy.start()
    for copy in note_copies:
        copy.wait_recv()

    row = lax.broadcasted_iota(jnp.int32, (dec, HD), 0).astype(jnp.float32)
    live = row < notes[0].astype(jnp.float32)[heads : heads + 1, :]
    key_live = lax.broadcasted_iota(jnp.int32, (dec, enc), 1) < memory_len[0, 0]

    def step(t, carry):
        squares = jnp.zeros((dec, HD), jnp.float32)
        for h in range(heads):
            x_h = held[:, h * HD : (h + 1) * HD].astype(jnp.float32)
            squares = squares + x_h * x_h
        mean = jnp.sum(squares, axis=-1, keepdims=True) * (1.0 / (heads * HD))
        scale = lax.rsqrt(mean + 1e-06)
        gains = notes[t].astype(jnp.float32)
        probs = []
        for h in range(heads):
            cols = slice(h * HD, (h + 1) * HD)
            q_h = (held[:, cols].astype(jnp.float32) * scale).astype(jnp.bfloat16)
            scores = lax.dot_general(
                q_h, kv[0, :, cols], (((1,), (1,)), ((), ())),
                preferred_element_type=jnp.float32,
            ) * HD ** (-0.5)
            scores = jnp.where(key_live, scores, jnp.float32(-1e30))
            expo = jnp.exp(scores - jnp.max(scores, axis=-1, keepdims=True))
            probs.append((expo / jnp.sum(expo, axis=-1, keepdims=True)).astype(jnp.bfloat16))
        for h in range(heads):
            cols = slice(h * HD, (h + 1) * HD)
            a_h = jnp.dot(
                probs[h], kv[1, :, cols], preferred_element_type=jnp.float32
            ).astype(jnp.bfloat16)
            mixed[t, :, cols] = a_h
            x_h = held[:, cols].astype(jnp.float32)
            moved = x_h + gains[h : h + 1, :] * a_h.astype(jnp.float32)
            held[:, cols] = jnp.where(live, moved, x_h).astype(jnp.bfloat16)
        return carry

    lax.fori_loop(0, STEPS, step, 0)

    final_copy = pltpu.make_async_remote_copy(
        src_ref=held, dst_ref=final.at[0, 0], send_sem=final_send, recv_sem=final_recv,
        device_id=section_at(STEPS - 1 - offset), device_id_type=MESH,
    )
    final_copy.start()

    part_copies = []
    for t in range(STEPS):
        cot_copies[t].wait_recv()
        for h in range(heads):
            cols = slice(h * HD, (h + 1) * HD)
            product = cots[t, :, cols].astype(jnp.float32) * mixed[t, :, cols].astype(jnp.float32)
            part[t, h : h + 1, :] = jnp.sum(
                jnp.where(live, product, jnp.float32(0.0)), axis=0, keepdims=True
            )
        copy = pltpu.make_async_remote_copy(
            src_ref=part.at[t], dst_ref=parts.at[t], send_sem=part_send.at[t],
            recv_sem=part_recv.at[t], device_id=section_at(t - offset), device_id_type=MESH,
        )
        copy.start()
        part_copies.append(copy)
    for copy in part_copies:
        copy.wait_recv()
    slots[rep] = (parts[0] + parts[1]) + parts[2]

    def slot_copy(j):
        return pltpu.make_async_remote_copy(
            src_ref=slots.at[rep], dst_ref=slots.at[rep], send_sem=slot_send.at[j],
            recv_sem=slot_recv.at[rep], device_id={"dp": lax.rem(rep + j, replicas)},
            device_id_type=MESH,
        )

    def give(j, carry):
        slot_copy(j).start()
        return carry

    def take(j, carry):
        other = lax.rem(rep + replicas - j, replicas)
        pltpu.make_async_remote_copy(
            src_ref=slots.at[other], dst_ref=slots.at[other], send_sem=slot_send.at[j],
            recv_sem=slot_recv.at[other], device_id={"dp": lax.rem(rep + j, replicas)},
            device_id_type=MESH,
        ).wait_recv()
        return carry

    lax.fori_loop(1, replicas, give, 0)
    lax.fori_loop(1, replicas, take, 0)
    total = lax.fori_loop(
        1, replicas, lambda r, total: total + slots[r], slots[0]
    )
    for h in range(heads):
        grad[:, h * HD : (h + 1) * HD] = total[h : h + 1, :]

    def sent(j, carry):
        slot_copy(j).wait_send()
        return carry

    lax.fori_loop(1, replicas, sent, 0)
    for copy in [x_copy, *note_copies, *cot_copies, *part_copies]:
        copy.wait_send()
    final_copy.wait()


def window(offset, sections, replicas, states, memory, memory_len, decode_len, gain, cotangent):
    dec, width = states.shape[2:]
    enc = memory.shape[3]
    heads = width // HD
    anywhere = pl.BlockSpec(memory_space=pl.ANY)
    scalar = pl.BlockSpec(memory_space=pltpu.SMEM)
    vector = pl.BlockSpec(memory_space=pltpu.VMEM)
    dma = pltpu.SemaphoreType.DMA
    return pl.pallas_call(
        functools.partial(window_kernel, offset, sections, replicas),
        out_shape=(
            jax.ShapeDtypeStruct(states.shape, jnp.bfloat16),
            jax.ShapeDtypeStruct((1, width), jnp.float32),
        ),
        in_specs=[anywhere, anywhere, scalar, scalar, vector, anywhere],
        out_specs=(anywhere, vector),
        scratch_shapes=[
            pltpu.VMEM((2, enc, width), jnp.bfloat16),
            pltpu.VMEM((dec, width), jnp.bfloat16),
            pltpu.VMEM((STEPS, dec, width), jnp.bfloat16),
            pltpu.VMEM((STEPS, dec, width), jnp.bfloat16),
            pltpu.VMEM((2 * heads, HD), jnp.bfloat16),
            pltpu.VMEM((STEPS, 2 * heads, HD), jnp.bfloat16),
            pltpu.VMEM((2 * heads, HD), jnp.float32),
            pltpu.VMEM((STEPS, heads, HD), jnp.float32),
            pltpu.VMEM((STEPS, heads, HD), jnp.float32),
            pltpu.VMEM((replicas, heads, HD), jnp.float32),
            dma, dma, dma, dma((STEPS,)), dma((STEPS,)), dma((STEPS,)), dma((STEPS,)),
            dma((STEPS,)), dma((STEPS,)), dma, dma, dma((replicas,)), dma((replicas,)),
        ],
        compiler_params=pltpu.CompilerParams(
            collective_id=offset, has_side_effects=True, vmem_limit_bytes=16 * 1024 * 1024
        ),
        cost_estimate=pl.CostEstimate(
            flops=STEPS * 4 * dec * enc * width,
            bytes_accessed=2 * (2 * enc + 5 * dec) * width,
            transcendentals=STEPS * heads * dec * enc,
        ),
        name="window",
    )(states, memory, memory_len, decode_len, gain, cotangent)


def solution(mesh):
    sections, replicas = mesh.shape["section"], mesh.shape["dp"]

    def per_device(states, memory, memory_len, decode_len, owner_map, section_gain, cotangent):
        branches = [
            functools.partial(window, offset, sections, replicas)
            for offset in range(STEPS, sections)
        ]
        return lax.switch(
            owner_map[0] - STEPS, branches,
            states, memory, memory_len, decode_len, section_gain, cotangent,
        )

    in_specs = (
        P("dp", "section", None, None),
        P("dp", "section", None, None, None),
        P("dp", "section"),
        P("dp", "section"),
        P(),
        P("section", None),
        P("dp", None, "section", None, None),
    )
    out_specs = (P("dp", "section", None, None), P("section", None))
    return jax.shard_map(
        per_device, mesh=mesh, in_specs=in_specs, out_specs=out_specs, check_vma=False
    )
```

```python
import functools

import jax
import jax.numpy as jnp
from jax import lax
from jax.experimental import pallas as pl
from jax.experimental.pallas import tpu as pltpu
from jax.sharding import PartitionSpec as P

HD = 256
STEPS = 3
MESH = pl.DeviceIdType.MESH


def heads_out(offset, heads):
    return [heads, 0 if offset % 2 else heads // 2, 0]


def window_kernel(
    offset, sections, replicas,
    states, memory, memory_len, decode_len, gain, cotangent,
    final, grad,
    kv, held, cots, own_cots, mixed, arrived, note, notes, rows_f32, part, parts, own, slots,
    kv_sem, own_sem, x_send, x_recv, cot_send, cot_recv, mixed_send, mixed_recv,
    note_send, note_recv, part_send, part_recv, final_send, final_recv, slot_send, slot_recv,
):
    me = lax.axis_index("section")
    rep = lax.axis_index("dp")
    heads = held.shape[1] // HD
    dec = held.shape[0]
    enc = kv.shape[1]
    outs = heads_out(offset, heads)

    def section_at(shift):
        return {"section": lax.rem(me + shift % sections, sections)}

    def to_section(src, dst, send, recv, shift):
        return pltpu.make_async_remote_copy(
            src_ref=src, dst_ref=dst, send_sem=send, recv_sem=recv,
            device_id=section_at(shift), device_id_type=MESH,
        )

    barrier = pltpu.get_barrier_semaphore()
    shifts = sorted({s % sections for t in range(STEPS) for s in (offset - t, t - offset)})
    for shift in shifts:
        pl.semaphore_signal(barrier, inc=1, device_id=section_at(shift), device_id_type=MESH)

    def greet(j, carry):
        pl.semaphore_signal(
            barrier, inc=1, device_id={"dp": lax.rem(rep + j, replicas)}, device_id_type=MESH
        )
        return carry

    lax.fori_loop(1, replicas, greet, 0)

    kv_copy = pltpu.make_async_copy(memory.at[0, 0], kv, kv_sem)
    kv_copy.start()

    for h in range(heads):
        rows_f32[h : h + 1, :] = gain[:, h * HD : (h + 1) * HD].astype(jnp.float32)
    rows_f32[heads:, :] = jnp.full((heads, HD), decode_len[0, 0], jnp.int32).astype(jnp.float32)
    note[...] = rows_f32[...].astype(jnp.bfloat16)

    x_copy = to_section(states.at[0, 0], held, x_send, x_recv, offset)
    note_copies = [
        to_section(note, notes.at[t], note_send.at[t], note_recv.at[t], offset - t)
        for t in range(STEPS)
    ]
    cot_copies, own_copies, mixed_copies, part_copies = {}, {}, {}, {}
    for t in range(STEPS):
        out = pl.ds(0, outs[t] * HD)
        rest = pl.ds(outs[t] * HD, (heads - outs[t]) * HD)
        rows = pl.ds(outs[t], heads - outs[t])
        if outs[t] > 0:
            own_copies[t] = pltpu.make_async_copy(
                cotangent.at[0, t, 0, :, out], own_cots.at[t, :, out], own_sem.at[t]
            )
            mixed_copies[t] = to_section(
                mixed.at[t, :, out], arrived.at[t, :, out],
                mixed_send.at[t], mixed_recv.at[t], t - offset,
            )
        if outs[t] < heads:
            cot_copies[t] = to_section(
                cotangent.at[0, t, 0, :, rest], cots.at[t, :, rest],
                cot_send.at[t], cot_recv.at[t], offset - t,
            )
            part_copies[t] = to_section(
                part.at[t, rows], parts.at[t, rows], part_send.at[t], part_recv.at[t], t - offset
            )
    final_copy = to_section(held, final.at[0, 0], final_send, final_recv, STEPS - 1 - offset)

    pl.semaphore_wait(barrier, len(shifts) + replicas - 1)
    x_copy.start()
    for copy in note_copies:
        copy.start()
    for copy in own_copies.values():
        copy.start()
    x_copy.wait_send()
    for t in sorted(cot_copies, reverse=True):
        cot_copies[t].start()

    kv_copy.wait()
    for copy in note_copies:
        copy.wait_recv()
    x_copy.wait_recv()

    row = lax.broadcasted_iota(jnp.int32, (dec, HD), 0).astype(jnp.float32)
    live = row < notes[0].astype(jnp.float32)[heads : heads + 1, :]
    key_live = lax.broadcasted_iota(jnp.int32, (dec, enc), 1) < memory_len[0, 0]

    def step(t, carry):
        squares = jnp.zeros((dec, HD), jnp.float32)
        for h in range(heads):
            x_h = held[:, h * HD : (h + 1) * HD].astype(jnp.float32)
            squares = squares + x_h * x_h
        mean = jnp.sum(squares, axis=-1, keepdims=True) * (1.0 / (heads * HD))
        scale = lax.rsqrt(mean + 1e-06)
        gains = notes[t].astype(jnp.float32)
        probs = []
        for h in range(heads):
            cols = slice(h * HD, (h + 1) * HD)
            q_h = (held[:, cols].astype(jnp.float32) * scale).astype(jnp.bfloat16)
            scores = lax.dot_general(
                q_h, kv[0, :, cols], (((1,), (1,)), ((), ())),
                preferred_element_type=jnp.float32,
            ) * HD ** (-0.5)
            scores = jnp.where(key_live, scores, jnp.float32(-1e30))
            expo = jnp.exp(scores - jnp.max(scores, axis=-1, keepdims=True))
            probs.append((expo / jnp.sum(expo, axis=-1, keepdims=True)).astype(jnp.bfloat16))
        for h in range(heads):
            cols = slice(h * HD, (h + 1) * HD)
            a_h = jnp.dot(probs[h], kv[1, :, cols], preferred_element_type=jnp.float32)
            a_h = jnp.where(live, a_h, jnp.float32(0.0)).astype(jnp.bfloat16)
            mixed[t, :, cols] = a_h
            x_h = held[:, cols].astype(jnp.float32)
            moved = x_h + gains[h : h + 1, :] * a_h.astype(jnp.float32)
            held[:, cols] = moved.astype(jnp.bfloat16)
        for at, copy in mixed_copies.items():
            pl.when(t == at)(copy.start)
        return carry

    lax.fori_loop(0, STEPS, step, 0)
    final_copy.start()

    def gradient(left, right, h):
        cols = slice(h * HD, (h + 1) * HD)
        product = left[:, cols].astype(jnp.float32) * right[:, cols].astype(jnp.float32)
        return jnp.sum(product, axis=0, keepdims=True)

    for t in sorted(cot_copies, reverse=True):
        cot_copies[t].wait_recv()
        for h in range(outs[t], heads):
            part[t, h : h + 1, :] = gradient(cots.at[t], mixed.at[t], h)
        part_copies[t].start()
    for t in sorted(mixed_copies):
        own_copies[t].wait()
        mixed_copies[t].wait_recv()
        for h in range(outs[t]):
            own[t, h : h + 1, :] = gradient(own_cots.at[t], arrived.at[t], h)
    for copy in part_copies.values():
        copy.wait_recv()
    shares = []
    for t in range(STEPS):
        pieces = []
        if outs[t] > 0:
            pieces.append(own[t, : outs[t], :])
        if outs[t] < heads:
            pieces.append(parts[t, outs[t] :, :])
        shares.append(pieces[0] if len(pieces) == 1 else jnp.concatenate(pieces, axis=0))
    slots[rep] = (shares[0] + shares[1]) + shares[2]

    def slot_copy(whose, j):
        return pltpu.make_async_remote_copy(
            src_ref=slots.at[whose], dst_ref=slots.at[whose], send_sem=slot_send.at[j],
            recv_sem=slot_recv.at[whose], device_id={"dp": lax.rem(rep + j, replicas)},
            device_id_type=MESH,
        )

    def give(j, carry):
        slot_copy(rep, j).start()
        return carry

    def take(j, carry):
        slot_copy(lax.rem(rep + replicas - j, replicas), j).wait_recv()
        return carry

    lax.fori_loop(1, replicas, give, 0)
    lax.fori_loop(1, replicas, take, 0)
    total = lax.fori_loop(1, replicas, lambda r, total: total + slots[r], slots[0])
    for h in range(heads):
        grad[:, h * HD : (h + 1) * HD] = total[h : h + 1, :]

    def sent(j, carry):
        slot_copy(rep, j).wait_send()
        return carry

    lax.fori_loop(1, replicas, sent, 0)
    for copy in [
        *note_copies, *cot_copies.values(), *mixed_copies.values(), *part_copies.values()
    ]:
        copy.wait_send()
    final_copy.wait()


def window(offset, sections, replicas, states, memory, memory_len, decode_len, gain, cotangent):
    dec, width = states.shape[2:]
    enc = memory.shape[3]
    heads = width // HD
    anywhere = pl.BlockSpec(memory_space=pl.ANY)
    scalar = pl.BlockSpec(memory_space=pltpu.SMEM)
    vector = pl.BlockSpec(memory_space=pltpu.VMEM)
    dma = pltpu.SemaphoreType.DMA
    return pl.pallas_call(
        functools.partial(window_kernel, offset, sections, replicas),
        out_shape=(
            jax.ShapeDtypeStruct(states.shape, jnp.bfloat16),
            jax.ShapeDtypeStruct((1, width), jnp.float32),
        ),
        in_specs=[anywhere, anywhere, scalar, scalar, vector, anywhere],
        out_specs=(anywhere, vector),
        scratch_shapes=[
            pltpu.VMEM((2, enc, width), jnp.bfloat16),
            pltpu.VMEM((dec, width), jnp.bfloat16),
            pltpu.VMEM((STEPS, dec, width), jnp.bfloat16),
            pltpu.VMEM((STEPS, dec, width), jnp.bfloat16),
            pltpu.VMEM((STEPS, dec, width), jnp.bfloat16),
            pltpu.VMEM((STEPS, dec, width), jnp.bfloat16),
            pltpu.VMEM((2 * heads, HD), jnp.bfloat16),
            pltpu.VMEM((STEPS, 2 * heads, HD), jnp.bfloat16),
            pltpu.VMEM((2 * heads, HD), jnp.float32),
            pltpu.VMEM((STEPS, heads, HD), jnp.float32),
            pltpu.VMEM((STEPS, heads, HD), jnp.float32),
            pltpu.VMEM((STEPS, heads, HD), jnp.float32),
            pltpu.VMEM((replicas, heads, HD), jnp.float32),
            dma, dma((STEPS,)), dma, dma, dma((STEPS,)), dma((STEPS,)), dma((STEPS,)),
            dma((STEPS,)), dma((STEPS,)), dma((STEPS,)), dma((STEPS,)), dma((STEPS,)),
            dma, dma, dma((replicas,)), dma((replicas,)),
        ],
        compiler_params=pltpu.CompilerParams(
            collective_id=offset, has_side_effects=True, vmem_limit_bytes=16 * 1024 * 1024
        ),
        cost_estimate=pl.CostEstimate(
            flops=STEPS * 4 * dec * enc * width,
            bytes_accessed=2 * (2 * enc + 5 * dec) * width,
            transcendentals=STEPS * heads * dec * enc,
        ),
        name=f"window_{offset}",
    )(states, memory, memory_len, decode_len, gain, cotangent)


def solution(mesh):
    sections, replicas = mesh.shape["section"], mesh.shape["dp"]

    def per_device(states, memory, memory_len, decode_len, owner_map, section_gain, cotangent):
        branches = [
            functools.partial(window, offset, sections, replicas)
            for offset in range(STEPS, sections)
        ]
        return lax.switch(
            owner_map[0] - STEPS, branches,
            states, memory, memory_len, decode_len, section_gain, cotangent,
        )

    in_specs = (
        P("dp", "section", None, None),
        P("dp", "section", None, None, None),
        P("dp", "section"),
        P("dp", "section"),
        P(),
        P("section", None),
        P("dp", None, "section", None, None),
    )
    out_specs = (P("dp", "section", None, None), P("section", None))
    return jax.shard_map(
        per_device, mesh=mesh, in_specs=in_specs, out_specs=out_specs, check_vma=False
    )
```

```python
import functools

import jax
import jax.numpy as jnp
from jax import lax
from jax.experimental import pallas as pl
from jax.experimental.pallas import tpu as pltpu
from jax.sharding import PartitionSpec as P

HD = 256
STEPS = 3
MESH = pl.DeviceIdType.MESH


WITH, LEFT, CAME = range(3)
PLANS = {
    3: ((0.5, 0.5, 0.5), (LEFT, CAME, CAME)),
    4: ((0.5, 0.5, 0), (LEFT, LEFT, WITH)),
    5: ((1, 0, 0), (WITH, WITH, LEFT)),
    6: ((0.5, 0.5, 0.5), (LEFT, CAME, LEFT)),
    7: ((1, 0, 0), (WITH, WITH, LEFT)),
}
OTHER = PLANS[4]


def window_kernel(
    offset, sections, replicas,
    states, memory, memory_len, decode_len, gain, cotangent,
    final, grad,
    kv, held, cots, own_cots, mixed, arrived, note, notes, rows_f32, part, parts, own, slots,
    kv_sem, own_sem, x_send, x_recv, cot_send, cot_recv, mixed_send, mixed_recv,
    note_send, note_recv, part_send, part_recv, final_send, final_recv, slot_send, slot_recv,
):
    me = lax.axis_index("section")
    rep = lax.axis_index("dp")
    heads = held.shape[1] // HD
    dec = held.shape[0]
    enc = kv.shape[1]
    shares_out, moments = PLANS[offset] if sections == 8 else OTHER
    outs = [int(share * heads) for share in shares_out]

    def cots_sent(moment):
        return [t for t in sorted(cot_copies, reverse=True) if moments[t] == moment]

    def section_at(shift):
        return {"section": lax.rem(me + shift % sections, sections)}

    def to_section(src, dst, send, recv, shift):
        return pltpu.make_async_remote_copy(
            src_ref=src, dst_ref=dst, send_sem=send, recv_sem=recv,
            device_id=section_at(shift), device_id_type=MESH,
        )

    barrier = pltpu.get_barrier_semaphore()
    shifts = sorted({s % sections for t in range(STEPS) for s in (offset - t, t - offset)})
    for shift in shifts:
        pl.semaphore_signal(barrier, inc=1, device_id=section_at(shift), device_id_type=MESH)

    def greet(j, carry):
        pl.semaphore_signal(
            barrier, inc=1, device_id={"dp": lax.rem(rep + j, replicas)}, device_id_type=MESH
        )
        return carry

    lax.fori_loop(1, replicas, greet, 0)

    kv_copy = pltpu.make_async_copy(memory.at[0, 0], kv, kv_sem)
    kv_copy.start()

    for h in range(heads):
        rows_f32[h : h + 1, :] = gain[:, h * HD : (h + 1) * HD].astype(jnp.float32)
    rows_f32[heads:, :] = jnp.full((heads, HD), decode_len[0, 0], jnp.int32).astype(jnp.float32)
    note[...] = rows_f32[...].astype(jnp.bfloat16)

    x_copy = to_section(states.at[0, 0], held, x_send, x_recv, offset)
    note_copies = [
        to_section(note, notes.at[t], note_send.at[t], note_recv.at[t], offset - t)
        for t in range(STEPS)
    ]
    cot_copies, own_copies, mixed_copies, part_copies = {}, {}, {}, {}
    for t in range(STEPS):
        out = pl.ds(0, outs[t] * HD)
        rest = pl.ds(outs[t] * HD, (heads - outs[t]) * HD)
        rows = pl.ds(outs[t], heads - outs[t])
        if outs[t] > 0:
            own_copies[t] = pltpu.make_async_copy(
                cotangent.at[0, t, 0, :, out], own_cots.at[t, :, out], own_sem.at[t]
            )
            mixed_copies[t] = to_section(
                mixed.at[t, :, out], arrived.at[t, :, out],
                mixed_send.at[t], mixed_recv.at[t], t - offset,
            )
        if outs[t] < heads:
            cot_copies[t] = to_section(
                cotangent.at[0, t, 0, :, rest], cots.at[t, :, rest],
                cot_send.at[t], cot_recv.at[t], offset - t,
            )
            part_copies[t] = to_section(
                part.at[t, rows], parts.at[t, rows], part_send.at[t], part_recv.at[t], t - offset
            )
    final_copy = to_section(held, final.at[0, 0], final_send, final_recv, STEPS - 1 - offset)

    pl.semaphore_wait(barrier, len(shifts) + replicas - 1)
    x_copy.start()
    for copy in note_copies:
        copy.start()
    for t in cots_sent(WITH):
        cot_copies[t].start()
    for copy in own_copies.values():
        copy.start()
    x_copy.wait_send()
    for t in cots_sent(LEFT):
        cot_copies[t].start()

    kv_copy.wait()
    for copy in note_copies:
        copy.wait_recv()
    x_copy.wait_recv()
    for t in cots_sent(CAME):
        cot_copies[t].start()

    row = lax.broadcasted_iota(jnp.int32, (dec, HD), 0).astype(jnp.float32)
    live = row < notes[0].astype(jnp.float32)[heads : heads + 1, :]
    key_live = lax.broadcasted_iota(jnp.int32, (dec, enc), 1) < memory_len[0, 0]

    def step(t, carry):
        squares = jnp.zeros((dec, HD), jnp.float32)
        for h in range(heads):
            x_h = held[:, h * HD : (h + 1) * HD].astype(jnp.float32)
            squares = squares + x_h * x_h
        mean = jnp.sum(squares, axis=-1, keepdims=True) * (1.0 / (heads * HD))
        scale = lax.rsqrt(mean + 1e-06)
        gains = notes[t].astype(jnp.float32)
        probs = []
        for h in range(heads):
            cols = slice(h * HD, (h + 1) * HD)
            q_h = (held[:, cols].astype(jnp.float32) * scale).astype(jnp.bfloat16)
            scores = lax.dot_general(
                q_h, kv[0, :, cols], (((1,), (1,)), ((), ())),
                preferred_element_type=jnp.float32,
            ) * HD ** (-0.5)
            scores = jnp.where(key_live, scores, jnp.float32(-1e30))
            expo = jnp.exp(scores - jnp.max(scores, axis=-1, keepdims=True))
            probs.append((expo / jnp.sum(expo, axis=-1, keepdims=True)).astype(jnp.bfloat16))
        for h in range(heads):
            cols = slice(h * HD, (h + 1) * HD)
            a_h = jnp.dot(probs[h], kv[1, :, cols], preferred_element_type=jnp.float32)
            a_h = jnp.where(live, a_h, jnp.float32(0.0)).astype(jnp.bfloat16)
            mixed[t, :, cols] = a_h
            x_h = held[:, cols].astype(jnp.float32)
            moved = x_h + gains[h : h + 1, :] * a_h.astype(jnp.float32)
            held[:, cols] = moved.astype(jnp.bfloat16)
        for at, copy in mixed_copies.items():
            pl.when(t == at)(copy.start)
        return carry

    lax.fori_loop(0, STEPS, step, 0)
    final_copy.start()

    def gradient(left, right, h):
        cols = slice(h * HD, (h + 1) * HD)
        product = left[:, cols].astype(jnp.float32) * right[:, cols].astype(jnp.float32)
        return jnp.sum(product, axis=0, keepdims=True)

    for t in sorted(cot_copies, reverse=True):
        cot_copies[t].wait_recv()
        for h in range(outs[t], heads):
            part[t, h : h + 1, :] = gradient(cots.at[t], mixed.at[t], h)
        part_copies[t].start()
    for t in sorted(mixed_copies):
        own_copies[t].wait()
        mixed_copies[t].wait_recv()
        for h in range(outs[t]):
            own[t, h : h + 1, :] = gradient(own_cots.at[t], arrived.at[t], h)
    for copy in part_copies.values():
        copy.wait_recv()
    shares = []
    for t in range(STEPS):
        pieces = []
        if outs[t] > 0:
            pieces.append(own[t, : outs[t], :])
        if outs[t] < heads:
            pieces.append(parts[t, outs[t] :, :])
        shares.append(pieces[0] if len(pieces) == 1 else jnp.concatenate(pieces, axis=0))
    slots[rep] = (shares[0] + shares[1]) + shares[2]

    def slot_copy(whose, j):
        return pltpu.make_async_remote_copy(
            src_ref=slots.at[whose], dst_ref=slots.at[whose], send_sem=slot_send.at[j],
            recv_sem=slot_recv.at[whose], device_id={"dp": lax.rem(rep + j, replicas)},
            device_id_type=MESH,
        )

    def give(j, carry):
        slot_copy(rep, j).start()
        return carry

    def take(j, carry):
        slot_copy(lax.rem(rep + replicas - j, replicas), j).wait_recv()
        return carry

    lax.fori_loop(1, replicas, give, 0)
    lax.fori_loop(1, replicas, take, 0)
    total = lax.fori_loop(1, replicas, lambda r, total: total + slots[r], slots[0])
    for h in range(heads):
        grad[:, h * HD : (h + 1) * HD] = total[h : h + 1, :]

    def sent(j, carry):
        slot_copy(rep, j).wait_send()
        return carry

    lax.fori_loop(1, replicas, sent, 0)
    for copy in [
        *note_copies, *cot_copies.values(), *mixed_copies.values(), *part_copies.values()
    ]:
        copy.wait_send()
    final_copy.wait()


def window(offset, sections, replicas, states, memory, memory_len, decode_len, gain, cotangent):
    dec, width = states.shape[2:]
    enc = memory.shape[3]
    heads = width // HD
    anywhere = pl.BlockSpec(memory_space=pl.ANY)
    scalar = pl.BlockSpec(memory_space=pltpu.SMEM)
    vector = pl.BlockSpec(memory_space=pltpu.VMEM)
    dma = pltpu.SemaphoreType.DMA
    return pl.pallas_call(
        functools.partial(window_kernel, offset, sections, replicas),
        out_shape=(
            jax.ShapeDtypeStruct(states.shape, jnp.bfloat16),
            jax.ShapeDtypeStruct((1, width), jnp.float32),
        ),
        in_specs=[anywhere, anywhere, scalar, scalar, vector, anywhere],
        out_specs=(anywhere, vector),
        scratch_shapes=[
            pltpu.VMEM((2, enc, width), jnp.bfloat16),
            pltpu.VMEM((dec, width), jnp.bfloat16),
            pltpu.VMEM((STEPS, dec, width), jnp.bfloat16),
            pltpu.VMEM((STEPS, dec, width), jnp.bfloat16),
            pltpu.VMEM((STEPS, dec, width), jnp.bfloat16),
            pltpu.VMEM((STEPS, dec, width), jnp.bfloat16),
            pltpu.VMEM((2 * heads, HD), jnp.bfloat16),
            pltpu.VMEM((STEPS, 2 * heads, HD), jnp.bfloat16),
            pltpu.VMEM((2 * heads, HD), jnp.float32),
            pltpu.VMEM((STEPS, heads, HD), jnp.float32),
            pltpu.VMEM((STEPS, heads, HD), jnp.float32),
            pltpu.VMEM((STEPS, heads, HD), jnp.float32),
            pltpu.VMEM((replicas, heads, HD), jnp.float32),
            dma, dma((STEPS,)), dma, dma, dma((STEPS,)), dma((STEPS,)), dma((STEPS,)),
            dma((STEPS,)), dma((STEPS,)), dma((STEPS,)), dma((STEPS,)), dma((STEPS,)),
            dma, dma, dma((replicas,)), dma((replicas,)),
        ],
        compiler_params=pltpu.CompilerParams(
            collective_id=offset, has_side_effects=True, vmem_limit_bytes=16 * 1024 * 1024
        ),
        cost_estimate=pl.CostEstimate(
            flops=STEPS * 4 * dec * enc * width,
            bytes_accessed=2 * (2 * enc + 5 * dec) * width,
            transcendentals=STEPS * heads * dec * enc,
        ),
        name=f"window_{offset}",
    )(states, memory, memory_len, decode_len, gain, cotangent)


def solution(mesh):
    sections, replicas = mesh.shape["section"], mesh.shape["dp"]

    def per_device(states, memory, memory_len, decode_len, owner_map, section_gain, cotangent):
        branches = [
            functools.partial(window, offset, sections, replicas)
            for offset in range(STEPS, sections)
        ]
        return lax.switch(
            owner_map[0] - STEPS, branches,
            states, memory, memory_len, decode_len, section_gain, cotangent,
        )

    in_specs = (
        P("dp", "section", None, None),
        P("dp", "section", None, None, None),
        P("dp", "section"),
        P("dp", "section"),
        P(),
        P("section", None),
        P("dp", None, "section", None, None),
    )
    out_specs = (P("dp", "section", None, None), P("section", None))
    return jax.shard_map(
        per_device, mesh=mesh, in_specs=in_specs, out_specs=out_specs, check_vma=False
    )
```

```python
import functools

import jax
import jax.numpy as jnp
from jax import lax
from jax.experimental import pallas as pl
from jax.experimental.pallas import tpu as pltpu
from jax.sharding import PartitionSpec as P

HD = 256
STEPS = 3
GROUP = 4
MESH = pl.DeviceIdType.MESH


WITH, LEFT, CAME = range(3)
PLANS = {
    3: ((0.5, 0.5, 0.5), (LEFT, CAME, CAME)),
    4: ((0.5, 0.5, 0), (LEFT, LEFT, WITH)),
    5: ((1, 0, 0), (WITH, WITH, LEFT)),
    6: ((0.5, 0.5, 0.5), (LEFT, CAME, LEFT)),
    7: ((1, 0, 0), (WITH, WITH, LEFT)),
}
OTHER = PLANS[4]


def window_kernel(
    offset, sections, replicas,
    states, memory, memory_len, decode_len, gain, cotangent,
    final, grad,
    kv, keys, scores, probs, held, cots, own_cots, mixed, arrived, note, notes, rows_f32, part, parts, own, slots,
    kv_sem, own_sem, x_send, x_recv, cot_send, cot_recv, mixed_send, mixed_recv,
    note_send, note_recv, part_send, part_recv, final_send, final_recv, slot_send, slot_recv,
):
    me = lax.axis_index("section")
    rep = lax.axis_index("dp")
    heads = held.shape[1] // HD
    dec = held.shape[0]
    enc = kv.shape[1]
    shares_out, moments = PLANS[offset] if sections == 8 else OTHER
    outs = [int(share * heads) for share in shares_out]

    def cots_sent(moment):
        return [t for t in sorted(cot_copies, reverse=True) if moments[t] == moment]

    def section_at(shift):
        return {"section": lax.rem(me + shift % sections, sections)}

    def to_section(src, dst, send, recv, shift):
        return pltpu.make_async_remote_copy(
            src_ref=src, dst_ref=dst, send_sem=send, recv_sem=recv,
            device_id=section_at(shift), device_id_type=MESH,
        )

    barrier = pltpu.get_barrier_semaphore()
    shifts = sorted({s % sections for t in range(STEPS) for s in (offset - t, t - offset)})
    for shift in shifts:
        pl.semaphore_signal(barrier, inc=1, device_id=section_at(shift), device_id_type=MESH)

    def greet(j, carry):
        pl.semaphore_signal(
            barrier, inc=1, device_id={"dp": lax.rem(rep + j, replicas)}, device_id_type=MESH
        )
        return carry

    lax.fori_loop(1, replicas, greet, 0)

    kv_copy = pltpu.make_async_copy(memory.at[0, 0], kv, kv_sem)
    kv_copy.start()

    for h in range(heads):
        rows_f32[h : h + 1, :] = gain[:, h * HD : (h + 1) * HD].astype(jnp.float32)
    rows_f32[heads:, :] = jnp.full((heads, HD), decode_len[0, 0], jnp.int32).astype(jnp.float32)
    note[...] = rows_f32[...].astype(jnp.bfloat16)

    x_copy = to_section(states.at[0, 0], held, x_send, x_recv, offset)
    note_copies = [
        to_section(note, notes.at[t], note_send.at[t], note_recv.at[t], offset - t)
        for t in range(STEPS)
    ]
    cot_copies, own_copies, mixed_copies, part_copies = {}, {}, {}, {}
    for t in range(STEPS):
        out = pl.ds(0, outs[t] * HD)
        rest = pl.ds(outs[t] * HD, (heads - outs[t]) * HD)
        rows = pl.ds(outs[t], heads - outs[t])
        if outs[t] > 0:
            own_copies[t] = pltpu.make_async_copy(
                cotangent.at[0, t, 0, :, out], own_cots.at[t, :, out], own_sem.at[t]
            )
            mixed_copies[t] = to_section(
                mixed.at[t, :, out], arrived.at[t, :, out],
                mixed_send.at[t], mixed_recv.at[t], t - offset,
            )
        if outs[t] < heads:
            cot_copies[t] = to_section(
                cotangent.at[0, t, 0, :, rest], cots.at[t, :, rest],
                cot_send.at[t], cot_recv.at[t], offset - t,
            )
            part_copies[t] = to_section(
                part.at[t, rows], parts.at[t, rows], part_send.at[t], part_recv.at[t], t - offset
            )
    final_copy = to_section(held, final.at[0, 0], final_send, final_recv, STEPS - 1 - offset)

    pl.semaphore_wait(barrier, len(shifts) + replicas - 1)
    x_copy.start()
    for copy in note_copies:
        copy.start()
    for t in cots_sent(WITH):
        cot_copies[t].start()
    for copy in own_copies.values():
        copy.start()
    x_copy.wait_send()
    for t in cots_sent(LEFT):
        cot_copies[t].start()

    kv_copy.wait()
    for h in range(heads):
        keys[h * HD : (h + 1) * HD, :] = jnp.transpose(kv[0, :, h * HD : (h + 1) * HD])
    for copy in note_copies:
        copy.wait_recv()
    x_copy.wait_recv()
    for t in cots_sent(CAME):
        cot_copies[t].start()

    row = lax.broadcasted_iota(jnp.int32, (dec, HD), 0).astype(jnp.float32)
    live = row < notes[0].astype(jnp.float32)[heads : heads + 1, :]
    key_live = lax.broadcasted_iota(jnp.int32, (GROUP * dec, enc), 1) < memory_len[0, 0]

    def step(t, carry):
        squares = jnp.zeros((dec, HD), jnp.float32)
        for h in range(heads):
            x_h = held[:, h * HD : (h + 1) * HD].astype(jnp.float32)
            squares = squares + x_h * x_h
        mean = jnp.sum(squares, axis=-1, keepdims=True) * (1.0 / (heads * HD))
        scale = lax.rsqrt(mean + 1e-06)
        gains = notes[t].astype(jnp.float32)
        for h in range(heads):
            cols = slice(h * HD, (h + 1) * HD)
            q_h = (held[:, cols].astype(jnp.float32) * scale).astype(jnp.bfloat16)
            scores[h * dec : (h + 1) * dec, :] = jnp.dot(
                q_h, keys[cols, :], preferred_element_type=jnp.float32
            )
        for first in range(0, heads * dec, GROUP * dec):
            rows = slice(first, first + GROUP * dec)
            masked = jnp.where(key_live, scores[rows, :] * HD ** (-0.5), jnp.float32(-1e30))
            expo = jnp.exp(masked - jnp.max(masked, axis=-1, keepdims=True))
            total = jnp.sum(expo, axis=-1, keepdims=True)
            probs[rows, :] = (expo / total).astype(jnp.bfloat16)
        for h in range(heads):
            cols = slice(h * HD, (h + 1) * HD)
            a_h = jnp.dot(
                probs[h * dec : (h + 1) * dec, :], kv[1, :, cols],
                preferred_element_type=jnp.float32,
            )
            a_h = jnp.where(live, a_h, jnp.float32(0.0)).astype(jnp.bfloat16)
            mixed[t, :, cols] = a_h
            x_h = held[:, cols].astype(jnp.float32)
            moved = x_h + gains[h : h + 1, :] * a_h.astype(jnp.float32)
            held[:, cols] = moved.astype(jnp.bfloat16)
        for at, copy in mixed_copies.items():
            pl.when(t == at)(copy.start)
        return carry

    lax.fori_loop(0, STEPS, step, 0)
    final_copy.start()

    def gradient(left, right, h):
        cols = slice(h * HD, (h + 1) * HD)
        product = left[:, cols].astype(jnp.float32) * right[:, cols].astype(jnp.float32)
        return jnp.sum(product, axis=0, keepdims=True)

    for t in sorted(cot_copies, reverse=True):
        cot_copies[t].wait_recv()
        for h in range(outs[t], heads):
            part[t, h : h + 1, :] = gradient(cots.at[t], mixed.at[t], h)
        part_copies[t].start()
    for t in sorted(mixed_copies):
        own_copies[t].wait()
        mixed_copies[t].wait_recv()
        for h in range(outs[t]):
            own[t, h : h + 1, :] = gradient(own_cots.at[t], arrived.at[t], h)
    for copy in part_copies.values():
        copy.wait_recv()
    shares = []
    for t in range(STEPS):
        pieces = []
        if outs[t] > 0:
            pieces.append(own[t, : outs[t], :])
        if outs[t] < heads:
            pieces.append(parts[t, outs[t] :, :])
        shares.append(pieces[0] if len(pieces) == 1 else jnp.concatenate(pieces, axis=0))
    slots[rep] = (shares[0] + shares[1]) + shares[2]

    def slot_copy(whose, j):
        return pltpu.make_async_remote_copy(
            src_ref=slots.at[whose], dst_ref=slots.at[whose], send_sem=slot_send.at[j],
            recv_sem=slot_recv.at[whose], device_id={"dp": lax.rem(rep + j, replicas)},
            device_id_type=MESH,
        )

    def give(j, carry):
        slot_copy(rep, j).start()
        return carry

    def take(j, carry):
        slot_copy(lax.rem(rep + replicas - j, replicas), j).wait_recv()
        return carry

    lax.fori_loop(1, replicas, give, 0)
    lax.fori_loop(1, replicas, take, 0)
    total = lax.fori_loop(1, replicas, lambda r, total: total + slots[r], slots[0])
    for h in range(heads):
        grad[:, h * HD : (h + 1) * HD] = total[h : h + 1, :]

    def sent(j, carry):
        slot_copy(rep, j).wait_send()
        return carry

    lax.fori_loop(1, replicas, sent, 0)
    for copy in [
        *note_copies, *cot_copies.values(), *mixed_copies.values(), *part_copies.values()
    ]:
        copy.wait_send()
    final_copy.wait()


def window(offset, sections, replicas, states, memory, memory_len, decode_len, gain, cotangent):
    dec, width = states.shape[2:]
    enc = memory.shape[3]
    heads = width // HD
    anywhere = pl.BlockSpec(memory_space=pl.ANY)
    scalar = pl.BlockSpec(memory_space=pltpu.SMEM)
    vector = pl.BlockSpec(memory_space=pltpu.VMEM)
    dma = pltpu.SemaphoreType.DMA
    return pl.pallas_call(
        functools.partial(window_kernel, offset, sections, replicas),
        out_shape=(
            jax.ShapeDtypeStruct(states.shape, jnp.bfloat16),
            jax.ShapeDtypeStruct((1, width), jnp.float32),
        ),
        in_specs=[anywhere, anywhere, scalar, scalar, vector, anywhere],
        out_specs=(anywhere, vector),
        scratch_shapes=[
            pltpu.VMEM((2, enc, width), jnp.bfloat16),
            pltpu.VMEM((width, enc), jnp.bfloat16),
            pltpu.VMEM((heads * dec, enc), jnp.float32),
            pltpu.VMEM((heads * dec, enc), jnp.bfloat16),
            pltpu.VMEM((dec, width), jnp.bfloat16),
            pltpu.VMEM((STEPS, dec, width), jnp.bfloat16),
            pltpu.VMEM((STEPS, dec, width), jnp.bfloat16),
            pltpu.VMEM((STEPS, dec, width), jnp.bfloat16),
            pltpu.VMEM((STEPS, dec, width), jnp.bfloat16),
            pltpu.VMEM((2 * heads, HD), jnp.bfloat16),
            pltpu.VMEM((STEPS, 2 * heads, HD), jnp.bfloat16),
            pltpu.VMEM((2 * heads, HD), jnp.float32),
            pltpu.VMEM((STEPS, heads, HD), jnp.float32),
            pltpu.VMEM((STEPS, heads, HD), jnp.float32),
            pltpu.VMEM((STEPS, heads, HD), jnp.float32),
            pltpu.VMEM((replicas, heads, HD), jnp.float32),
            dma, dma((STEPS,)), dma, dma, dma((STEPS,)), dma((STEPS,)), dma((STEPS,)),
            dma((STEPS,)), dma((STEPS,)), dma((STEPS,)), dma((STEPS,)), dma((STEPS,)),
            dma, dma, dma((replicas,)), dma((replicas,)),
        ],
        compiler_params=pltpu.CompilerParams(
            collective_id=offset, has_side_effects=True, vmem_limit_bytes=16 * 1024 * 1024
        ),
        cost_estimate=pl.CostEstimate(
            flops=STEPS * 4 * dec * enc * width,
            bytes_accessed=2 * (2 * enc + 5 * dec) * width,
            transcendentals=STEPS * heads * dec * enc,
        ),
        name=f"window_{offset}",
    )(states, memory, memory_len, decode_len, gain, cotangent)


def solution(mesh):
    sections, replicas = mesh.shape["section"], mesh.shape["dp"]

    def per_device(states, memory, memory_len, decode_len, owner_map, section_gain, cotangent):
        branches = [
            functools.partial(window, offset, sections, replicas)
            for offset in range(STEPS, sections)
        ]
        return lax.switch(
            owner_map[0] - STEPS, branches,
            states, memory, memory_len, decode_len, section_gain, cotangent,
        )

    in_specs = (
        P("dp", "section", None, None),
        P("dp", "section", None, None, None),
        P("dp", "section"),
        P("dp", "section"),
        P(),
        P("section", None),
        P("dp", None, "section", None, None),
    )
    out_specs = (P("dp", "section", None, None), P("section", None))
    return jax.shard_map(
        per_device, mesh=mesh, in_specs=in_specs, out_specs=out_specs, check_vma=False
    )
```

```python
import functools

import jax
import jax.numpy as jnp
from jax import lax
from jax.experimental import pallas as pl
from jax.experimental.pallas import tpu as pltpu
from jax.sharding import PartitionSpec as P

HD = 256
STEPS = 3
GROUP = 4
MESH = pl.DeviceIdType.MESH


WITH, LEFT, CAME = range(3)
PLANS = {
    3: ((0.5, 0.5, 0.5), (LEFT, CAME, CAME)),
    4: ((0.5, 0.5, 0), (LEFT, LEFT, WITH)),
    5: ((1, 0, 0), (WITH, WITH, LEFT)),
    6: ((0.5, 0.5, 0.5), (LEFT, CAME, LEFT)),
    7: ((1, 0, 0), (WITH, WITH, LEFT)),
}
OTHER = PLANS[4]


def window_kernel(
    offset, sections, replicas,
    states, memory, memory_len, decode_len, gain, cotangent,
    final, grad,
    kv, keys, scores, probs, held, cots, own_cots, mixed, arrived, note, notes, rows_f32, part, parts, own, slots,
    kv_sem, own_sem, x_send, x_recv, cot_send, cot_recv, mixed_send, mixed_recv,
    note_send, note_recv, part_send, part_recv, final_send, final_recv, slot_send, slot_recv,
):
    me = lax.axis_index("section")
    rep = lax.axis_index("dp")
    heads = held.shape[1] // HD
    dec = held.shape[0]
    enc = kv.shape[1]
    shares_out, moments = PLANS[offset] if sections == 8 else OTHER
    outs = [int(share * heads) for share in shares_out]

    def cots_sent(moment):
        return [t for t in sorted(cot_copies, reverse=True) if moments[t] == moment]

    def section_at(shift):
        return {"section": lax.rem(me + shift % sections, sections)}

    def to_section(src, dst, send, recv, shift):
        return pltpu.make_async_remote_copy(
            src_ref=src, dst_ref=dst, send_sem=send, recv_sem=recv,
            device_id=section_at(shift), device_id_type=MESH,
        )

    barrier = pltpu.get_barrier_semaphore()
    shifts = sorted({s % sections for t in range(STEPS) for s in (offset - t, t - offset)})
    for shift in shifts:
        pl.semaphore_signal(barrier, inc=1, device_id=section_at(shift), device_id_type=MESH)

    def greet(j, carry):
        pl.semaphore_signal(
            barrier, inc=1, device_id={"dp": lax.rem(rep + j, replicas)}, device_id_type=MESH
        )
        return carry

    lax.fori_loop(1, replicas, greet, 0)

    kv_copy = pltpu.make_async_copy(memory.at[0, 0], kv, kv_sem)
    kv_copy.start()

    for h in range(heads):
        rows_f32[h : h + 1, :] = gain[:, h * HD : (h + 1) * HD].astype(jnp.float32)
    rows_f32[heads:, :] = jnp.full((heads, HD), decode_len[0, 0], jnp.int32).astype(jnp.float32)
    note[...] = rows_f32[...].astype(jnp.bfloat16)

    half = heads // 2
    halves = [pl.ds(i * half * HD, half * HD) for i in range(2)]
    x_copies = [
        to_section(states.at[0, 0, :, cols], held.at[:, cols], x_send.at[i], x_recv.at[i], offset)
        for i, cols in enumerate(halves)
    ]
    note_copies = []
    for t in range(STEPS):
        rows = pl.ds(0, 2 * heads if t == 0 else heads)
        note_copies.append(to_section(
            note.at[rows], notes.at[t, rows], note_send.at[t], note_recv.at[t], offset - t
        ))
    cot_copies, own_copies, mixed_copies, part_copies = {}, {}, {}, {}
    for t in range(STEPS):
        out = pl.ds(0, outs[t] * HD)
        rest = pl.ds(outs[t] * HD, (heads - outs[t]) * HD)
        rows = pl.ds(outs[t], heads - outs[t])
        if outs[t] > 0:
            own_copies[t] = pltpu.make_async_copy(
                cotangent.at[0, t, 0, :, out], own_cots.at[t, :, out], own_sem.at[t]
            )
            for i in range(outs[t] // half):
                mixed_copies[t, i] = to_section(
                    mixed.at[t, :, halves[i]], arrived.at[t, :, halves[i]],
                    mixed_send.at[t, i], mixed_recv.at[t, i], t - offset,
                )
        if outs[t] < heads:
            cot_copies[t] = to_section(
                cotangent.at[0, t, 0, :, rest], cots.at[t, :, rest],
                cot_send.at[t], cot_recv.at[t], offset - t,
            )
            part_copies[t] = to_section(
                part.at[t, rows], parts.at[t, rows], part_send.at[t], part_recv.at[t], t - offset
            )
    final_copies = [
        to_section(
            held.at[:, cols], final.at[0, 0, :, cols],
            final_send.at[i], final_recv.at[i], STEPS - 1 - offset,
        )
        for i, cols in enumerate(halves)
    ]

    pl.semaphore_wait(barrier, len(shifts) + replicas - 1)
    for copy in x_copies:
        copy.start()
    for copy in note_copies:
        copy.start()
    for t in cots_sent(WITH):
        cot_copies[t].start()
    for copy in own_copies.values():
        copy.start()
    for copy in x_copies:
        copy.wait_send()
    for t in cots_sent(LEFT):
        cot_copies[t].start()

    kv_copy.wait()
    for h in range(heads):
        keys[h * HD : (h + 1) * HD, :] = jnp.transpose(kv[0, :, h * HD : (h + 1) * HD])
    for copy in note_copies:
        copy.wait_recv()
    for copy in x_copies:
        copy.wait_recv()
    for t in cots_sent(CAME):
        cot_copies[t].start()

    row = lax.broadcasted_iota(jnp.int32, (dec, HD), 0).astype(jnp.float32)
    live = row < notes[0].astype(jnp.float32)[heads : heads + 1, :]
    key_live = lax.broadcasted_iota(jnp.int32, (GROUP * dec, enc), 1) < memory_len[0, 0]

    def step(t, carry):
        squares = jnp.zeros((dec, HD), jnp.float32)
        for h in range(heads):
            x_h = held[:, h * HD : (h + 1) * HD].astype(jnp.float32)
            squares = squares + x_h * x_h
        mean = jnp.sum(squares, axis=-1, keepdims=True) * (1.0 / (heads * HD))
        scale = lax.rsqrt(mean + 1e-06)
        gains = notes[t, :heads, :].astype(jnp.float32)
        for h in range(heads):
            cols = slice(h * HD, (h + 1) * HD)
            q_h = (held[:, cols].astype(jnp.float32) * scale).astype(jnp.bfloat16)
            scores[h * dec : (h + 1) * dec, :] = jnp.dot(
                q_h, keys[cols, :], preferred_element_type=jnp.float32
            )
        for first in range(0, heads * dec, GROUP * dec):
            rows = slice(first, first + GROUP * dec)
            masked = jnp.where(key_live, scores[rows, :] * HD ** (-0.5), jnp.float32(-1e30))
            expo = jnp.exp(masked - jnp.max(masked, axis=-1, keepdims=True))
            total = jnp.sum(expo, axis=-1, keepdims=True)
            probs[rows, :] = (expo / total).astype(jnp.bfloat16)
        for h in range(heads):
            cols = slice(h * HD, (h + 1) * HD)
            a_h = jnp.dot(
                probs[h * dec : (h + 1) * dec, :], kv[1, :, cols],
                preferred_element_type=jnp.float32,
            )
            a_h = jnp.where(live, a_h, jnp.float32(0.0)).astype(jnp.bfloat16)
            mixed[t, :, cols] = a_h
            x_h = held[:, cols].astype(jnp.float32)
            moved = x_h + gains[h : h + 1, :] * a_h.astype(jnp.float32)
            held[:, cols] = moved.astype(jnp.bfloat16)
            if (h + 1) % half == 0:
                for (at, i), copy in mixed_copies.items():
                    if i == h // half:
                        pl.when(t == at)(copy.start)
                pl.when(t == STEPS - 1)(final_copies[h // half].start)
        return carry

    lax.fori_loop(0, STEPS, step, 0)

    def gradient(left, right, h):
        cols = slice(h * HD, (h + 1) * HD)
        product = left[:, cols].astype(jnp.float32) * right[:, cols].astype(jnp.float32)
        return jnp.sum(product, axis=0, keepdims=True)

    for t in sorted(cot_copies, reverse=True):
        cot_copies[t].wait_recv()
        for h in range(outs[t], heads):
            part[t, h : h + 1, :] = gradient(cots.at[t], mixed.at[t], h)
        part_copies[t].start()
    for t in sorted(own_copies):
        own_copies[t].wait()
        for h in range(outs[t]):
            if h % half == 0:
                mixed_copies[t, h // half].wait_recv()
            own[t, h : h + 1, :] = gradient(own_cots.at[t], arrived.at[t], h)
    for copy in part_copies.values():
        copy.wait_recv()
    shares = []
    for t in range(STEPS):
        pieces = []
        if outs[t] > 0:
            pieces.append(own[t, : outs[t], :])
        if outs[t] < heads:
            pieces.append(parts[t, outs[t] :, :])
        shares.append(pieces[0] if len(pieces) == 1 else jnp.concatenate(pieces, axis=0))
    slots[rep] = (shares[0] + shares[1]) + shares[2]

    def slot_copy(whose, j):
        return pltpu.make_async_remote_copy(
            src_ref=slots.at[whose], dst_ref=slots.at[whose], send_sem=slot_send.at[j],
            recv_sem=slot_recv.at[whose], device_id={"dp": lax.rem(rep + j, replicas)},
            device_id_type=MESH,
        )

    def give(j, carry):
        slot_copy(rep, j).start()
        return carry

    def take(j, carry):
        slot_copy(lax.rem(rep + replicas - j, replicas), j).wait_recv()
        return carry

    lax.fori_loop(1, replicas, give, 0)
    lax.fori_loop(1, replicas, take, 0)
    total = lax.fori_loop(1, replicas, lambda r, total: total + slots[r], slots[0])
    for h in range(heads):
        grad[:, h * HD : (h + 1) * HD] = total[h : h + 1, :]

    def sent(j, carry):
        slot_copy(rep, j).wait_send()
        return carry

    lax.fori_loop(1, replicas, sent, 0)
    for copy in [
        *note_copies, *cot_copies.values(), *mixed_copies.values(), *part_copies.values()
    ]:
        copy.wait_send()
    for copy in final_copies:
        copy.wait()


def window(offset, sections, replicas, states, memory, memory_len, decode_len, gain, cotangent):
    dec, width = states.shape[2:]
    enc = memory.shape[3]
    heads = width // HD
    anywhere = pl.BlockSpec(memory_space=pl.ANY)
    scalar = pl.BlockSpec(memory_space=pltpu.SMEM)
    vector = pl.BlockSpec(memory_space=pltpu.VMEM)
    dma = pltpu.SemaphoreType.DMA
    return pl.pallas_call(
        functools.partial(window_kernel, offset, sections, replicas),
        out_shape=(
            jax.ShapeDtypeStruct(states.shape, jnp.bfloat16),
            jax.ShapeDtypeStruct((1, width), jnp.float32),
        ),
        in_specs=[anywhere, anywhere, scalar, scalar, vector, anywhere],
        out_specs=(anywhere, vector),
        scratch_shapes=[
            pltpu.VMEM((2, enc, width), jnp.bfloat16),
            pltpu.VMEM((width, enc), jnp.bfloat16),
            pltpu.VMEM((heads * dec, enc), jnp.float32),
            pltpu.VMEM((heads * dec, enc), jnp.bfloat16),
            pltpu.VMEM((dec, width), jnp.bfloat16),
            pltpu.VMEM((STEPS, dec, width), jnp.bfloat16),
            pltpu.VMEM((STEPS, dec, width), jnp.bfloat16),
            pltpu.VMEM((STEPS, dec, width), jnp.bfloat16),
            pltpu.VMEM((STEPS, dec, width), jnp.bfloat16),
            pltpu.VMEM((2 * heads, HD), jnp.bfloat16),
            pltpu.VMEM((STEPS, 2 * heads, HD), jnp.bfloat16),
            pltpu.VMEM((2 * heads, HD), jnp.float32),
            pltpu.VMEM((STEPS, heads, HD), jnp.float32),
            pltpu.VMEM((STEPS, heads, HD), jnp.float32),
            pltpu.VMEM((STEPS, heads, HD), jnp.float32),
            pltpu.VMEM((replicas, heads, HD), jnp.float32),
            dma, dma((STEPS,)), dma((2,)), dma((2,)), dma((STEPS,)), dma((STEPS,)),
            dma((STEPS, 2)), dma((STEPS, 2)), dma((STEPS,)), dma((STEPS,)), dma((STEPS,)),
            dma((STEPS,)), dma((2,)), dma((2,)), dma((replicas,)), dma((replicas,)),
        ],
        compiler_params=pltpu.CompilerParams(
            collective_id=offset, has_side_effects=True, vmem_limit_bytes=16 * 1024 * 1024
        ),
        cost_estimate=pl.CostEstimate(
            flops=STEPS * 4 * dec * enc * width,
            bytes_accessed=2 * (2 * enc + 5 * dec) * width,
            transcendentals=STEPS * heads * dec * enc,
        ),
        name=f"window_{offset}",
    )(states, memory, memory_len, decode_len, gain, cotangent)


def solution(mesh):
    sections, replicas = mesh.shape["section"], mesh.shape["dp"]

    def per_device(states, memory, memory_len, decode_len, owner_map, section_gain, cotangent):
        branches = [
            functools.partial(window, offset, sections, replicas)
            for offset in range(STEPS, sections)
        ]
        return lax.switch(
            owner_map[0] - STEPS, branches,
            states, memory, memory_len, decode_len, section_gain, cotangent,
        )

    in_specs = (
        P("dp", "section", None, None),
        P("dp", "section", None, None, None),
        P("dp", "section"),
        P("dp", "section"),
        P(),
        P("section", None),
        P("dp", None, "section", None, None),
    )
    out_specs = (P("dp", "section", None, None), P("section", None))
    return jax.shard_map(
        per_device, mesh=mesh, in_specs=in_specs, out_specs=out_specs, check_vma=False
    )
```

```python
import functools

import jax
import jax.numpy as jnp
from jax import lax
from jax.experimental import pallas as pl
from jax.experimental.pallas import tpu as pltpu
from jax.sharding import PartitionSpec as P

HD = 256
STEPS = 3
GROUP = 4
MESH = pl.DeviceIdType.MESH


WITH, LEFT, CAME = range(3)
PLANS = {
    3: ((1, 0, 0), (WITH, CAME, LEFT)),
    4: ((0.5, 0.5, 0), (LEFT, LEFT, WITH)),
    5: ((1, 0, 0), (WITH, WITH, LEFT)),
    6: ((0.5, 0.5, 0.5), (LEFT, CAME, LEFT)),
    7: ((1, 0, 0), (WITH, WITH, LEFT)),
}
OTHER = PLANS[4]


def window_kernel(
    offset, sections, replicas,
    states, memory, memory_len, decode_len, gain, cotangent,
    final, grad,
    kv, keys, scores, probs, held, cots, own_cots, mixed, arrived, note, notes, rows_f32, part, parts, own, slots,
    kv_sem, own_sem, x_send, x_recv, cot_send, cot_recv, mixed_send, mixed_recv,
    note_send, note_recv, part_send, part_recv, final_send, final_recv, slot_send, slot_recv,
):
    me = lax.axis_index("section")
    rep = lax.axis_index("dp")
    heads = held.shape[1] // HD
    dec = held.shape[0]
    enc = kv.shape[1]
    shares_out, moments = PLANS[offset] if sections == 8 else OTHER
    outs = [int(share * heads) for share in shares_out]

    def cots_sent(moment):
        return [t for t in sorted(cot_copies, reverse=True) if moments[t] == moment]

    def section_at(shift):
        return {"section": lax.rem(me + shift % sections, sections)}

    def to_section(src, dst, send, recv, shift):
        return pltpu.make_async_remote_copy(
            src_ref=src, dst_ref=dst, send_sem=send, recv_sem=recv,
            device_id=section_at(shift), device_id_type=MESH,
        )

    barrier = pltpu.get_barrier_semaphore()
    shifts = sorted({s % sections for t in range(STEPS) for s in (offset - t, t - offset)})
    for shift in shifts:
        pl.semaphore_signal(barrier, inc=1, device_id=section_at(shift), device_id_type=MESH)

    def greet(j, carry):
        pl.semaphore_signal(
            barrier, inc=1, device_id={"dp": lax.rem(rep + j, replicas)}, device_id_type=MESH
        )
        return carry

    lax.fori_loop(1, replicas, greet, 0)

    kv_copy = pltpu.make_async_copy(memory.at[0, 0], kv, kv_sem)
    kv_copy.start()

    for h in range(heads):
        rows_f32[h : h + 1, :] = gain[:, h * HD : (h + 1) * HD].astype(jnp.float32)
    rows_f32[heads:, :] = jnp.full((heads, HD), decode_len[0, 0], jnp.int32).astype(jnp.float32)
    note[...] = rows_f32[...].astype(jnp.bfloat16)

    half = heads // 2
    halves = [pl.ds(i * half * HD, half * HD) for i in range(2)]
    x_copies = [
        to_section(states.at[0, 0, :, cols], held.at[:, cols], x_send.at[i], x_recv.at[i], offset)
        for i, cols in enumerate(halves)
    ]
    note_copies = []
    for t in range(STEPS):
        rows = pl.ds(0, 2 * heads if t == 0 else heads)
        note_copies.append(to_section(
            note.at[rows], notes.at[t, rows], note_send.at[t], note_recv.at[t], offset - t
        ))
    cot_copies, own_copies, mixed_copies, part_copies = {}, {}, {}, {}
    for t in range(STEPS):
        out = pl.ds(0, outs[t] * HD)
        rest = pl.ds(outs[t] * HD, (heads - outs[t]) * HD)
        rows = pl.ds(outs[t], heads - outs[t])
        if outs[t] > 0:
            own_copies[t] = pltpu.make_async_copy(
                cotangent.at[0, t, 0, :, out], own_cots.at[t, :, out], own_sem.at[t]
            )
            for i in range(outs[t] // half):
                mixed_copies[t, i] = to_section(
                    mixed.at[t, :, halves[i]], arrived.at[t, :, halves[i]],
                    mixed_send.at[t, i], mixed_recv.at[t, i], t - offset,
                )
        if outs[t] < heads:
            cot_copies[t] = to_section(
                cotangent.at[0, t, 0, :, rest], cots.at[t, :, rest],
                cot_send.at[t], cot_recv.at[t], offset - t,
            )
            part_copies[t] = to_section(
                part.at[t, rows], parts.at[t, rows], part_send.at[t], part_recv.at[t], t - offset
            )
    final_copies = [
        to_section(
            held.at[:, cols], final.at[0, 0, :, cols],
            final_send.at[i], final_recv.at[i], STEPS - 1 - offset,
        )
        for i, cols in enumerate(halves)
    ]

    pl.semaphore_wait(barrier, len(shifts) + replicas - 1)
    for copy in x_copies:
        copy.start()
    for copy in note_copies:
        copy.start()
    for t in cots_sent(WITH):
        cot_copies[t].start()
    for copy in own_copies.values():
        copy.start()
    for copy in x_copies:
        copy.wait_send()
    for t in cots_sent(LEFT):
        cot_copies[t].start()

    kv_copy.wait()
    for h in range(heads):
        keys[h * HD : (h + 1) * HD, :] = jnp.transpose(kv[0, :, h * HD : (h + 1) * HD])
    for copy in note_copies:
        copy.wait_recv()
    for copy in x_copies:
        copy.wait_recv()
    for t in cots_sent(CAME):
        cot_copies[t].start()

    row = lax.broadcasted_iota(jnp.int32, (dec, HD), 0).astype(jnp.float32)
    live = row < notes[0].astype(jnp.float32)[heads : heads + 1, :]
    key_live = lax.broadcasted_iota(jnp.int32, (GROUP * dec, enc), 1) < memory_len[0, 0]

    def step(t, carry):
        squares = jnp.zeros((dec, HD), jnp.float32)
        for h in range(heads):
            x_h = held[:, h * HD : (h + 1) * HD].astype(jnp.float32)
            squares = squares + x_h * x_h
        mean = jnp.sum(squares, axis=-1, keepdims=True) * (1.0 / (heads * HD))
        scale = lax.rsqrt(mean + 1e-06)
        gains = notes[t, :heads, :].astype(jnp.float32)
        for h in range(heads):
            cols = slice(h * HD, (h + 1) * HD)
            q_h = (held[:, cols].astype(jnp.float32) * scale).astype(jnp.bfloat16)
            scores[h * dec : (h + 1) * dec, :] = jnp.dot(
                q_h, keys[cols, :], preferred_element_type=jnp.float32
            )
        for first in range(0, heads * dec, GROUP * dec):
            rows = slice(first, first + GROUP * dec)
            masked = jnp.where(key_live, scores[rows, :] * HD ** (-0.5), jnp.float32(-1e30))
            expo = jnp.exp(masked - jnp.max(masked, axis=-1, keepdims=True))
            total = jnp.sum(expo, axis=-1, keepdims=True)
            probs[rows, :] = (expo / total).astype(jnp.bfloat16)
        for h in range(heads):
            cols = slice(h * HD, (h + 1) * HD)
            a_h = jnp.dot(
                probs[h * dec : (h + 1) * dec, :], kv[1, :, cols],
                preferred_element_type=jnp.float32,
            )
            a_h = jnp.where(live, a_h, jnp.float32(0.0)).astype(jnp.bfloat16)
            mixed[t, :, cols] = a_h
            x_h = held[:, cols].astype(jnp.float32)
            moved = x_h + gains[h : h + 1, :] * a_h.astype(jnp.float32)
            held[:, cols] = moved.astype(jnp.bfloat16)
            if (h + 1) % half == 0:
                for (at, i), copy in mixed_copies.items():
                    if i == h // half:
                        pl.when(t == at)(copy.start)
                pl.when(t == STEPS - 1)(final_copies[h // half].start)
        return carry

    lax.fori_loop(0, STEPS, step, 0)

    def gradient(left, right, h):
        cols = slice(h * HD, (h + 1) * HD)
        product = left[:, cols].astype(jnp.float32) * right[:, cols].astype(jnp.float32)
        return jnp.sum(product, axis=0, keepdims=True)

    for t in sorted(cot_copies, reverse=True):
        cot_copies[t].wait_recv()
        for h in range(outs[t], heads):
            part[t, h : h + 1, :] = gradient(cots.at[t], mixed.at[t], h)
        part_copies[t].start()
    for t in sorted(own_copies):
        own_copies[t].wait()
        for h in range(outs[t]):
            if h % half == 0:
                mixed_copies[t, h // half].wait_recv()
            own[t, h : h + 1, :] = gradient(own_cots.at[t], arrived.at[t], h)
    for copy in part_copies.values():
        copy.wait_recv()
    shares = []
    for t in range(STEPS):
        pieces = []
        if outs[t] > 0:
            pieces.append(own[t, : outs[t], :])
        if outs[t] < heads:
            pieces.append(parts[t, outs[t] :, :])
        shares.append(pieces[0] if len(pieces) == 1 else jnp.concatenate(pieces, axis=0))
    slots[rep] = (shares[0] + shares[1]) + shares[2]

    def slot_copy(whose, j):
        return pltpu.make_async_remote_copy(
            src_ref=slots.at[whose], dst_ref=slots.at[whose], send_sem=slot_send.at[j],
            recv_sem=slot_recv.at[whose], device_id={"dp": lax.rem(rep + j, replicas)},
            device_id_type=MESH,
        )

    def give(j, carry):
        slot_copy(rep, j).start()
        return carry

    def take(j, carry):
        slot_copy(lax.rem(rep + replicas - j, replicas), j).wait_recv()
        return carry

    lax.fori_loop(1, replicas, give, 0)
    lax.fori_loop(1, replicas, take, 0)
    total = lax.fori_loop(1, replicas, lambda r, total: total + slots[r], slots[0])
    for h in range(heads):
        grad[:, h * HD : (h + 1) * HD] = total[h : h + 1, :]

    def sent(j, carry):
        slot_copy(rep, j).wait_send()
        return carry

    lax.fori_loop(1, replicas, sent, 0)
    for copy in [
        *note_copies, *cot_copies.values(), *mixed_copies.values(), *part_copies.values()
    ]:
        copy.wait_send()
    for copy in final_copies:
        copy.wait()


def window(offset, sections, replicas, states, memory, memory_len, decode_len, gain, cotangent):
    dec, width = states.shape[2:]
    enc = memory.shape[3]
    heads = width // HD
    anywhere = pl.BlockSpec(memory_space=pl.ANY)
    scalar = pl.BlockSpec(memory_space=pltpu.SMEM)
    vector = pl.BlockSpec(memory_space=pltpu.VMEM)
    dma = pltpu.SemaphoreType.DMA
    return pl.pallas_call(
        functools.partial(window_kernel, offset, sections, replicas),
        out_shape=(
            jax.ShapeDtypeStruct(states.shape, jnp.bfloat16),
            jax.ShapeDtypeStruct((1, width), jnp.float32),
        ),
        in_specs=[anywhere, anywhere, scalar, scalar, vector, anywhere],
        out_specs=(anywhere, vector),
        scratch_shapes=[
            pltpu.VMEM((2, enc, width), jnp.bfloat16),
            pltpu.VMEM((width, enc), jnp.bfloat16),
            pltpu.VMEM((heads * dec, enc), jnp.float32),
            pltpu.VMEM((heads * dec, enc), jnp.bfloat16),
            pltpu.VMEM((dec, width), jnp.bfloat16),
            pltpu.VMEM((STEPS, dec, width), jnp.bfloat16),
            pltpu.VMEM((STEPS, dec, width), jnp.bfloat16),
            pltpu.VMEM((STEPS, dec, width), jnp.bfloat16),
            pltpu.VMEM((STEPS, dec, width), jnp.bfloat16),
            pltpu.VMEM((2 * heads, HD), jnp.bfloat16),
            pltpu.VMEM((STEPS, 2 * heads, HD), jnp.bfloat16),
            pltpu.VMEM((2 * heads, HD), jnp.float32),
            pltpu.VMEM((STEPS, heads, HD), jnp.float32),
            pltpu.VMEM((STEPS, heads, HD), jnp.float32),
            pltpu.VMEM((STEPS, heads, HD), jnp.float32),
            pltpu.VMEM((replicas, heads, HD), jnp.float32),
            dma, dma((STEPS,)), dma((2,)), dma((2,)), dma((STEPS,)), dma((STEPS,)),
            dma((STEPS, 2)), dma((STEPS, 2)), dma((STEPS,)), dma((STEPS,)), dma((STEPS,)),
            dma((STEPS,)), dma((2,)), dma((2,)), dma((replicas,)), dma((replicas,)),
        ],
        compiler_params=pltpu.CompilerParams(
            collective_id=offset, has_side_effects=True, vmem_limit_bytes=16 * 1024 * 1024
        ),
        cost_estimate=pl.CostEstimate(
            flops=STEPS * 4 * dec * enc * width,
            bytes_accessed=2 * (2 * enc + 5 * dec) * width,
            transcendentals=STEPS * heads * dec * enc,
        ),
        name=f"window_{offset}",
    )(states, memory, memory_len, decode_len, gain, cotangent)


def solution(mesh):
    sections, replicas = mesh.shape["section"], mesh.shape["dp"]

    def per_device(states, memory, memory_len, decode_len, owner_map, section_gain, cotangent):
        branches = [
            functools.partial(window, offset, sections, replicas)
            for offset in range(STEPS, sections)
        ]
        return lax.switch(
            owner_map[0] - STEPS, branches,
            states, memory, memory_len, decode_len, section_gain, cotangent,
        )

    in_specs = (
        P("dp", "section", None, None),
        P("dp", "section", None, None, None),
        P("dp", "section"),
        P("dp", "section"),
        P(),
        P("section", None),
        P("dp", None, "section", None, None),
    )
    out_specs = (P("dp", "section", None, None), P("section", None))
    return jax.shard_map(
        per_device, mesh=mesh, in_specs=in_specs, out_specs=out_specs, check_vma=False
    )
```
